32 devices in a mesh: tx: 8 (over y, x, core), ty: 4 (over z).
Axes of the slice: x: 2, y: 2, z: 4, core: 2. Of those that a mesh axis runs over, the one named last changes fastest.
Arguments:
- adjoint_in: float32 [5, 3, 64, 64, 128], P(None, None, 'ty', 'tx'), may hold values from -6 to 6
- courant: float32 [2, 3, 64, 64, 128], P(None, None, 'ty', 'tx'), may hold values from -0.45 to 0.45
- vertical_inverse: float32 [5, 128, 128], replicated, as said below
- links: int32 [40, 4], replicated, may hold values from 0 to 95, as said below
Outputs:
- adjoint_out: float32 [5, 3, 64, 64, 128], P(None, None, 'ty', 'tx')
The draws below stay inside these ranges and needn't reach their ends.
Inputs may be any that keep to these rules, and one draw needn't show every extreme that they name: `links`: the three panel slots hold three faces of a cube that meet at one corner, in an order drawn afresh; call them X, Y, Z. X's east side joins Y's west side (code 0, both ways, tile row to same tile row), X's north side joins Z's south side (code 1, both ways, tile column to same tile column), Y's north side joins Z's east side with rotation: cell x = i of Y's top row is the neighbour of cell y = i of Z's east column (code 2 for Z's east ghosts, two rows a tile with off 0 and 8; code 3 for Y's north ghosts, one row a tile with off 0 or 8); all other panel sides are open. Row order is drawn afresh. Offsets are 0 or 8, codes 0 to 3. `vertical_inverse`: each block has a diagonal in [0.6, 1.0) and independent off-diagonal entries.
All inputs are finite; a program needn't handle non-finite values.
Results may differ from the reference program's by a relative error of at most 0.0003.
Values sent between devices are 32-bit elements; how exact they have to be, the bound alone decides.
A program may use at most 64 MiB of HBM per device.

```python
import math
import jax
import jax.numpy as jnp
from jax import lax

S = 5
P_SIZE = 3
L = 128
STEPS = 2
CX = 8
CY = 16
TCOLS = 8
TROWS = 4
NX = 64
NY = 64
NLINKS = 40


def draw_vertical_inverse(key, part):
    spread = 0.45 / math.sqrt(L)
    others = jax.random.normal(jax.random.fold_in(key, 5), (S, L, L), jnp.float32) * spread
    diagonal = jax.random.uniform(jax.random.fold_in(key, 6), (S, L), jnp.float32, 0.6, 1.0)
    identity = jnp.eye(L, dtype=jnp.float32)
    return others * (1.0 - identity) + diagonal[:, :, None] * identity


def draw_links(key, part):
    order = jax.random.permutation(jax.random.fold_in(key, 11), 3).astype(jnp.int32)
    face_x = order[0]
    face_y = order[1]
    face_z = order[2]
    tile_count = TCOLS * TROWS
    last_col = TCOLS - 1
    last_row = TROWS - 1
    row_ids = jnp.arange(TROWS, dtype=jnp.int32)
    col_ids = jnp.arange(TCOLS, dtype=jnp.int32)
    row_zeros = jnp.zeros((TROWS,), jnp.int32)
    col_zeros = jnp.zeros((TCOLS,), jnp.int32)

    def tile_id(slot, column, row):
        return slot * tile_count + row * TCOLS + column
    blocks = [jnp.stack([tile_id(face_y, row_zeros, row_ids), tile_id(face_x, row_zeros + last_col, row_ids), row_zeros, row_zeros], axis=1), jnp.stack([tile_id(face_x, row_zeros + last_col, row_ids), tile_id(face_y, row_zeros, row_ids), row_zeros, row_zeros], axis=1), jnp.stack([tile_id(face_z, col_ids, col_zeros), tile_id(face_x, col_ids, col_zeros + last_row), col_zeros, col_zeros + 1], axis=1), jnp.stack([tile_id(face_x, col_ids, col_zeros + last_row), tile_id(face_z, col_ids, col_zeros), col_zeros, col_zeros + 1], axis=1), jnp.stack([tile_id(face_y, col_ids, col_zeros + last_row), tile_id(face_z, col_zeros + last_col, col_ids // 2), col_ids % 2 * CX, col_zeros + 2], axis=1), jnp.stack([tile_id(face_z, col_zeros + last_col, col_ids // 2), tile_id(face_y, col_ids, col_zeros + last_row), col_ids % 2 * CX, col_zeros + 3], axis=1)]
    table_rows = jnp.concatenate(blocks, axis=0).astype(jnp.int32)
    shuffle = jax.random.permutation(jax.random.fold_in(key, 12), NLINKS)
    return table_rows[shuffle]


def shard_levels(own_key, extent, cuts, least, largest):
    level = 1.0
    for dim, parts in cuts:
        steps = jax.random.uniform(jax.random.fold_in(jax.random.fold_in(own_key, 6), dim), (parts,), jnp.float32, least / len(cuts), largest / len(cuts))
        level = level * jnp.repeat(jnp.exp(steps), extent[dim] // parts).reshape((-1,) + (1,) * (len(extent) - 1 - dim))
    return level


def normal_values(rng, dims, scale, reach, split=(), kind=jnp.bfloat16):
    factor_of = shard_levels(rng, dims, split, -0.22, 0.18) if split else 1.0
    entries = jax.random.normal(rng, dims, jnp.float32) * scale * factor_of
    return jnp.minimum(jnp.maximum(entries, -reach), reach).astype(kind)


def setup_inputs(seed: int = 0) -> dict:
    splits = jax.random.split(jax.random.key(seed), 5)
    return {
        "adjoint_in": normal_values(splits[0], (S, P_SIZE, NY, NX, L), 1.0, 6.0, ((2, 4), (3, 8)), jnp.float32),
        "courant": jnp.clip(jax.random.uniform(splits[1], (2, P_SIZE, NY, NX, L), jnp.float32, -0.45, 0.45) * shard_levels(splits[1], (2, P_SIZE, NY, NX, L), ((2, 4), (3, 8)), -0.4, 0.0), -0.45, 0.45),
        "vertical_inverse": draw_vertical_inverse(jax.random.fold_in(splits[4], 71), 0),
        "links": draw_links(jax.random.fold_in(splits[4], 71), 0),
    }


def fill_ghosts(tracer, links):
    padded = jnp.pad(tracer, ((0, 0), (1, 1), (1, 1), (0, 0)))
    tile_count = TCOLS * TROWS

    def place_link(current, link_row):
        zero_index = jnp.zeros((), jnp.int32)
        src_slot = (link_row[0] // tile_count).astype(jnp.int32)
        src_col = (link_row[0] % tile_count % TCOLS).astype(jnp.int32)
        src_row = (link_row[0] % tile_count // TCOLS).astype(jnp.int32)
        dst_slot = (link_row[1] // tile_count).astype(jnp.int32)
        dst_col = (link_row[1] % tile_count % TCOLS).astype(jnp.int32)
        dst_row = (link_row[1] % tile_count // TCOLS).astype(jnp.int32)
        offset = link_row[2].astype(jnp.int32)

        def aligned_x(target):
            src_x = jnp.where(src_col == 0, zero_index, zero_index + NX - 1)
            dst_x = jnp.where(dst_col == 0, zero_index, zero_index + NX + 1)
            strip = lax.dynamic_slice(tracer, (src_slot, src_row * CY, src_x, zero_index), (1, CY, 1, L))
            return lax.dynamic_update_slice(target, strip, (dst_slot, dst_row * CY + 1, dst_x, zero_index))

        def aligned_y(target):
            src_y = jnp.where(src_row == 0, zero_index, zero_index + NY - 1)
            dst_y = jnp.where(dst_row == 0, zero_index, zero_index + NY + 1)
            strip = lax.dynamic_slice(tracer, (src_slot, src_y, src_col * CX, zero_index), (1, 1, CX, L))
            return lax.dynamic_update_slice(target, strip, (dst_slot, dst_y, dst_col * CX + 1, zero_index))

        def rotated_east(target):
            strip = lax.dynamic_slice(tracer, (src_slot, zero_index + NY - 1, src_col * CX, zero_index), (1, 1, CX, L))
            strip = strip.reshape((1, CX, 1, L))
            return lax.dynamic_update_slice(target, strip, (dst_slot, dst_row * CY + offset + 1, zero_index + NX + 1, zero_index))

        def rotated_north(target):
            strip = lax.dynamic_slice(tracer, (src_slot, src_row * CY + offset, zero_index + NX - 1, zero_index), (1, CX, 1, L))
            strip = strip.reshape((1, 1, CX, L))
            return lax.dynamic_update_slice(target, strip, (dst_slot, zero_index + NY + 1, dst_col * CX + 1, zero_index))
        updated = lax.switch(link_row[3].astype(jnp.int32), [aligned_x, aligned_y, rotated_east, rotated_north], current)
        return (updated, None)
    padded, _ = lax.scan(place_link, padded, links)
    return padded

def model_step(tracer, courant, inverse, links):
    padded = fill_ghosts(tracer, links)
    east_side = padded[:, 1:-1, 2:]
    west_side = padded[:, 1:-1, :-2]
    north_side = padded[:, 2:, 1:-1]
    south_side = padded[:, :-2, 1:-1]
    advected = tracer - 0.5 * courant[0] * (east_side - west_side) - 0.5 * courant[1] * (north_side - south_side)
    return jnp.einsum('lm,kyxm->kyxl', inverse, advected, precision=lax.Precision.HIGHEST)

def reference(adjoint_in, courant, vertical_inverse, links):

    def per_species(species_args):
        adjoint, inverse = species_args

        def forward(tracer):
            return model_step(tracer, courant, inverse, links)
        _, pullback = jax.vjp(forward, jnp.zeros_like(adjoint))
        for step_index in range(STEPS):
            adjoint = pullback(adjoint)[0]
        return adjoint
    return lax.map(per_species, (adjoint_in, vertical_inverse))
```

```python
import functools

import jax
import jax.numpy as jnp
from jax import lax
from jax.experimental import pallas as pl
from jax.experimental.pallas import tpu as pltpu
from jax.sharding import PartitionSpec as P

STEPS = 2
EAST, WEST, NORTH, SOUTH = range(4)


def kernel(
    species, slots, cells_y, cells_x, cols, rows,
    adj_ref, courant_ref, inverse_ref, links_ref, out_ref,
    mid, mixed, sent, received, to_turn_n, to_turn_e, from_turn_e, from_turn_n,
    send_sems, recv_sems, turn_send, turn_recv,
):
    ratio = cells_y // cells_x
    tile_count = cols * rows
    col = lax.axis_index("tx")
    row = lax.axis_index("ty")
    at_east, at_west = col == cols - 1, col == 0
    at_north, at_south = row == rows - 1, row == 0
    seam = (at_east, at_west, at_north, at_south)
    far_seam = (at_west, at_east, at_south, at_north)
    east, west = lax.rem(col + 1, cols), lax.rem(col + cols - 1, cols)
    north, south = lax.rem(row + 1, rows), lax.rem(row + rows - 1, rows)
    targets = ({"tx": east}, {"tx": west}, {"ty": north}, {"ty": south})
    turn_row = lax.div(col * cells_x, cells_y)
    turn_part = lax.rem(col, ratio)
    north_turns = {"tx": cols - 1, "ty": turn_row}
    north_remote = at_north & jnp.logical_not(at_east)
    east_turns = [{"tx": row * ratio + j, "ty": rows - 1} for j in range(ratio)]
    corner = at_east & at_north
    east_remote = [
        at_east & jnp.logical_not(at_north) if j == ratio - 1 else at_east for j in range(ratio)
    ]

    barrier = pltpu.get_barrier_semaphore()

    def greet(device):
        pl.semaphore_signal(
            barrier, inc=1, device_id=device, device_id_type=pl.DeviceIdType.MESH
        )

    for device in targets:
        greet(device)

    @pl.when(north_remote)
    def _():
        greet(north_turns)

    for j in range(ratio):

        @pl.when(east_remote[j])
        def _(j=j):
            greet(east_turns[j])

    def read_link(index, faces):
        turned = links_ref[index, 3] == 2
        source = lax.div(links_ref[index, 0], tile_count)
        target = lax.div(links_ref[index, 1], tile_count)
        return jnp.where(turned, source, faces[0]), jnp.where(turned, target, faces[1])

    zero = jnp.int32(0)
    face_y, face_z = lax.fori_loop(0, links_ref.shape[0], read_link, (zero, zero))
    face_x = jnp.clip(slots - face_y - face_z, 0, slots - 1)
    face_y = jnp.clip(face_y, 0, slots - 1)
    face_z = jnp.clip(face_z, 0, slots - 1)

    def weight(face, slot, value):
        return jnp.where(face == slot, jnp.float32(value), jnp.float32(0.0))

    first_col = pl.ds(0, cells_y, stride=cells_x)
    last_col = pl.ds(cells_x - 1, cells_y, stride=cells_x)
    first_row = pl.ds(0, cells_x)
    last_row = pl.ds((cells_y - 1) * cells_x, cells_x)
    strips = (last_col, first_col, last_row, first_row)
    seam_faces = (face_x, face_y, face_x, face_z)

    def outgoing(step, side):
        return sent[step][side]

    def incoming(step, side):
        return received[step][side]

    def halo_copy(step, side, short):
        source, target = outgoing(step, side), incoming(step, side)
        if short:
            source, target = source.at[pl.ds(0, species)], target.at[pl.ds(0, species)]
        return pltpu.make_async_remote_copy(
            src_ref=source,
            dst_ref=target,
            send_sem=send_sems.at[step, side],
            recv_sem=recv_sems.at[step, side],
            device_id=targets[side],
            device_id_type=pl.DeviceIdType.MESH,
        )

    def north_copy(step, part):
        return pltpu.make_async_remote_copy(
            src_ref=to_turn_n[step],
            dst_ref=from_turn_e[step][part],
            send_sem=turn_send.at[step, ratio],
            recv_sem=turn_recv.at[step, part],
            device_id=north_turns,
            device_id_type=pl.DeviceIdType.MESH,
        )

    def east_copy(step, part):
        return pltpu.make_async_remote_copy(
            src_ref=to_turn_e[step][part],
            dst_ref=from_turn_n[step],
            send_sem=turn_send.at[step, part],
            recv_sem=turn_recv.at[step, ratio],
            device_id=east_turns[part],
            device_id_type=pl.DeviceIdType.MESH,
        )

    def either(condition, act):
        pl.when(condition)(functools.partial(act, True))
        pl.when(jnp.logical_not(condition))(functools.partial(act, False))

    lane_x = lax.broadcasted_iota(jnp.int32, (cells_y, cells_x, mixed.shape[-1]), 1)

    for step in range(STEPS):
        source = adj_ref if step == 0 else mid
        target = mid if step < STEPS - 1 else out_ref

        @pl.loop(0, species)
        def _(s):
            base = s * slots
            values = source[pl.ds(base, slots)].reshape(slots * cells_y * cells_x, -1)
            high = values.astype(jnp.bfloat16)
            low = (values - high.astype(jnp.float32)).astype(jnp.bfloat16)
            inverse = inverse_ref[s]
            inverse_high = inverse.astype(jnp.bfloat16)
            inverse_low = (inverse - inverse_high.astype(jnp.float32)).astype(jnp.bfloat16)
            both = jnp.concatenate([inverse_high, inverse_low], axis=1)
            product = jnp.dot(
                jnp.concatenate([high, low], axis=1),
                jnp.concatenate([both, both], axis=0),
                preferred_element_type=jnp.float32,
            )
            levels = inverse.shape[-1]
            product = product[:, :levels] + product[:, levels:]
            mixed[pl.ds(base, slots)] = product.reshape(slots, cells_y * cells_x, levels)
            for k in range(slots):
                for side in range(4):
                    strip = strips[side]
                    flux = courant_ref[side // 2, k, strip, :] * mixed[base + k, strip, :]
                    outgoing(step, side)[base + k] = flux

        for side in range(4):

            @pl.when(seam[side])
            def _(side=side):
                strip, face = strips[side], seam_faces[side]
                factor = courant_ref[side // 2, face, strip, :]
                for s in range(species):
                    outgoing(step, side)[s] = factor * mixed[s * slots + face, strip, :]

        @pl.when(at_north)
        def _():
            factor = courant_ref[1, face_y, last_row, :]
            for s in range(species):
                to_turn_n[step][s] = factor * mixed[s * slots + face_y, last_row, :]

        @pl.when(at_east)
        def _():
            for j in range(ratio):
                strip = pl.ds(j * cells_x * cells_x + cells_x - 1, cells_x, stride=cells_x)
                factor = courant_ref[0, face_z, strip, :]
                for s in range(species):
                    to_turn_e[step][j][s] = factor * mixed[s * slots + face_z, strip, :]

        if step == 0:
            peers = 4 + sum(c.astype(jnp.int32) for c in [north_remote, *east_remote])
            pl.semaphore_wait(barrier, peers)

        for j in range(ratio):

            @pl.when(north_remote & (turn_part == j))
            def _(j=j):
                north_copy(step, j).start()

            @pl.when(east_remote[j])
            def _(j=j):
                east_copy(step, j).start()

        for side in range(4):
            either(seam[side], lambda short, side=side: halo_copy(step, side, short).start())

        @pl.when(corner)
        def _():
            from_turn_e[step][ratio - 1][...] = to_turn_n[step][...]
            from_turn_n[step][...] = to_turn_e[step][ratio - 1][...]

        @pl.loop(0, species)
        def _(s):
            for k in range(slots):
                here = mixed[s * slots + k].reshape(cells_y, cells_x, -1)
                along_x = 0.5 * courant_ref[0, k].reshape(here.shape) * here
                along_y = 0.5 * courant_ref[1, k].reshape(here.shape) * here
                ahead = jnp.where(
                    lane_x == cells_x - 1, 0.0, pltpu.roll(along_x, cells_x - 1, 1)
                )
                behind = jnp.where(lane_x == 0, 0.0, pltpu.roll(along_x, 1, 1))
                nothing = jnp.zeros_like(along_y[:1])
                above = jnp.concatenate([along_y[1:], nothing], axis=0)
                below = jnp.concatenate([nothing, along_y[:-1]], axis=0)
                result = here + (ahead - behind) + (above - below)
                target[s * slots + k] = result.reshape(cells_y * cells_x, -1)

        for side in range(4):
            either(
                far_seam[side], lambda short, side=side: halo_copy(step, side, short).wait_recv()
            )

        @pl.when(at_east)
        def _():
            for j in range(ratio):
                if j < ratio - 1:
                    north_copy(step, j).wait_recv()
                else:

                    @pl.when(east_remote[j])
                    def _():
                        north_copy(step, ratio - 1).wait_recv()

        @pl.when(north_remote)
        def _():
            east_copy(step, 0).wait_recv()

        boundary = (first_col, last_col, first_row, last_row)
        sign = (-0.5, 0.5, -0.5, 0.5)
        filled = (face_y, face_x, face_z, face_x)
        for side in range(4):
            strip = boundary[side]

            @pl.when(jnp.logical_not(far_seam[side]))
            def _(side=side, strip=strip):
                @pl.loop(0, species)
                def _(s):
                    for k in range(slots):
                        index = s * slots + k
                        ghost = incoming(step, side)[index]
                        target[index, strip, :] = target[index, strip, :] + sign[side] * ghost

            @pl.when(far_seam[side])
            def _(side=side, strip=strip):
                @pl.loop(0, species)
                def _(s):
                    ghost = incoming(step, side)[s]
                    for k in range(slots):
                        index = s * slots + k
                        value = target[index, strip, :]
                        value = value + weight(filled[side], k, sign[side]) * ghost
                        if side == WEST:
                            turned = jnp.concatenate(
                                [from_turn_e[step][j][s] for j in range(ratio)], axis=0
                            )
                            value = value - weight(face_z, k, 0.5) * turned
                        if side == SOUTH:
                            value = value - weight(face_y, k, 0.5) * from_turn_n[step][s]
                        target[index, strip, :] = value

    for step in range(STEPS):
        for side in range(4):
            either(seam[side], lambda short, side=side: halo_copy(step, side, short).wait_send())

        for j in range(ratio):

            @pl.when(north_remote & (turn_part == j))
            def _(j=j):
                north_copy(step, j).wait_send()

            @pl.when(east_remote[j])
            def _(j=j):
                east_copy(step, j).wait_send()


def on_device(adjoint_in, courant, vertical_inverse, links):
    cols, rows = lax.axis_size("tx"), lax.axis_size("ty")
    species, slots, cells_y, cells_x, levels = adjoint_in.shape
    ratio = cells_y // cells_x
    planes, cells = species * slots, cells_y * cells_x
    vmem = pl.BlockSpec(memory_space=pltpu.VMEM)

    def buffer(*shape):
        return pltpu.VMEM(shape + (levels,), jnp.float32)

    halo = [buffer(planes, cells_y)] * 2 + [buffer(planes, cells_x)] * 2
    turn = buffer(species, cells_x)
    result = pl.pallas_call(
        functools.partial(kernel, species, slots, cells_y, cells_x, cols, rows),
        out_shape=jax.ShapeDtypeStruct((planes, cells, levels), jnp.float32),
        in_specs=[vmem, vmem, vmem, pl.BlockSpec(memory_space=pltpu.SMEM)],
        out_specs=vmem,
        scratch_shapes=[
            buffer(planes, cells),
            buffer(planes, cells),
            [halo] * STEPS,
            [halo] * STEPS,
            [turn] * STEPS,
            [[turn] * ratio] * STEPS,
            [[turn] * ratio] * STEPS,
            [turn] * STEPS,
            pltpu.SemaphoreType.DMA((STEPS, 4)),
            pltpu.SemaphoreType.DMA((STEPS, 4)),
            pltpu.SemaphoreType.DMA((STEPS, ratio + 1)),
            pltpu.SemaphoreType.DMA((STEPS, ratio + 1)),
        ],
        compiler_params=pltpu.CompilerParams(
            collective_id=0, has_side_effects=True, vmem_limit_bytes=32 * 1024 * 1024
        ),
    )(
        adjoint_in.reshape(planes, cells, levels),
        courant.reshape(2, slots, cells, levels),
        vertical_inverse,
        links,
    )
    return result.reshape(adjoint_in.shape)


def solution(mesh):
    placed = (P(None, None, "ty", "tx", None), P(None, None, "ty", "tx", None), P(), P())
    return jax.shard_map(
        on_device,
        mesh=mesh,
        in_specs=placed,
        out_specs=P(None, None, "ty", "tx", None),
        check_vma=False,
    )
```

```python
import functools

import jax
import jax.numpy as jnp
from jax import lax
from jax.experimental import pallas as pl
from jax.experimental.pallas import tpu as pltpu
from jax.sharding import PartitionSpec as P

STEPS = 2
EAST, WEST, NORTH, SOUTH = range(4)


def kernel(
    species, slots, cells_y, cells_x, cols, rows,
    adj_hbm, courant_hbm, inverse_hbm, links_hbm, out_ref,
    adj_ref, courant_ref, inverse_ref, links_ref,
    mid, mixed, sent, received, to_turn_n, to_turn_e, from_turn_e, from_turn_n,
    send_sems, recv_sems, turn_send, turn_recv, load_sems,
):
    ratio = cells_y // cells_x
    tile_count = cols * rows
    col = lax.axis_index("tx")
    row = lax.axis_index("ty")
    at_east, at_west = col == cols - 1, col == 0
    at_north, at_south = row == rows - 1, row == 0
    seam = (at_east, at_west, at_north, at_south)
    far_seam = (at_west, at_east, at_south, at_north)
    east, west = lax.rem(col + 1, cols), lax.rem(col + cols - 1, cols)
    north, south = lax.rem(row + 1, rows), lax.rem(row + rows - 1, rows)
    targets = ({"tx": east}, {"tx": west}, {"ty": north}, {"ty": south})
    turn_row = lax.div(col * cells_x, cells_y)
    turn_part = lax.rem(col, ratio)
    north_turns = {"tx": cols - 1, "ty": turn_row}
    north_remote = at_north & jnp.logical_not(at_east)
    east_turns = [{"tx": row * ratio + j, "ty": rows - 1} for j in range(ratio)]
    corner = at_east & at_north
    east_remote = [
        at_east & jnp.logical_not(at_north) if j == ratio - 1 else at_east for j in range(ratio)
    ]

    barrier = pltpu.get_barrier_semaphore()

    def greet(device):
        pl.semaphore_signal(
            barrier, inc=1, device_id=device, device_id_type=pl.DeviceIdType.MESH
        )

    for device in targets:
        greet(device)

    @pl.when(north_remote)
    def _():
        greet(north_turns)

    for j in range(ratio):

        @pl.when(east_remote[j])
        def _(j=j):
            greet(east_turns[j])

    loads = [
        pltpu.make_async_copy(links_hbm, links_ref, load_sems.at[0]),
        pltpu.make_async_copy(inverse_hbm, inverse_ref, load_sems.at[1]),
    ]
    for s in range(species):
        planes = pl.ds(s * slots, slots)
        loads.append(
            pltpu.make_async_copy(adj_hbm.at[planes], adj_ref.at[planes], load_sems.at[3 + s])
        )
    loads.append(pltpu.make_async_copy(courant_hbm, courant_ref, load_sems.at[2]))
    for load in loads:
        load.start()
    loads[0].wait()

    def read_link(index, tiles):
        turned = links_ref[3, index] == 2
        return (
            jnp.where(turned, links_ref[0, index], tiles[0]),
            jnp.where(turned, links_ref[1, index], tiles[1]),
        )

    zero = jnp.int32(0)
    tile_y, tile_z = lax.fori_loop(0, links_ref.shape[1], read_link, (zero, zero))
    face_y, face_z = lax.div(tile_y, tile_count), lax.div(tile_z, tile_count)
    face_x = jnp.clip(slots - face_y - face_z, 0, slots - 1)
    face_y = jnp.clip(face_y, 0, slots - 1)
    face_z = jnp.clip(face_z, 0, slots - 1)

    def weight(face, slot, value):
        return jnp.where(face == slot, jnp.float32(value), jnp.float32(0.0))

    first_col = pl.ds(0, cells_y, stride=cells_x)
    last_col = pl.ds(cells_x - 1, cells_y, stride=cells_x)
    first_row = pl.ds(0, cells_x)
    last_row = pl.ds((cells_y - 1) * cells_x, cells_x)
    strips = (last_col, first_col, last_row, first_row)
    seam_faces = (face_x, face_y, face_x, face_z)

    def outgoing(step, side):
        return sent[step][side]

    def incoming(step, side):
        return received[step][side]

    def halo_copy(step, side, short):
        source, target = outgoing(step, side), incoming(step, side)
        if short:
            source, target = source.at[pl.ds(0, species)], target.at[pl.ds(0, species)]
        return pltpu.make_async_remote_copy(
            src_ref=source,
            dst_ref=target,
            send_sem=send_sems.at[step, side],
            recv_sem=recv_sems.at[step, side],
            device_id=targets[side],
            device_id_type=pl.DeviceIdType.MESH,
        )

    def north_copy(step, part):
        return pltpu.make_async_remote_copy(
            src_ref=to_turn_n[step],
            dst_ref=from_turn_e[step][part],
            send_sem=turn_send.at[step, ratio],
            recv_sem=turn_recv.at[step, part],
            device_id=north_turns,
            device_id_type=pl.DeviceIdType.MESH,
        )

    def east_copy(step, part):
        return pltpu.make_async_remote_copy(
            src_ref=to_turn_e[step][part],
            dst_ref=from_turn_n[step],
            send_sem=turn_send.at[step, part],
            recv_sem=turn_recv.at[step, ratio],
            device_id=east_turns[part],
            device_id_type=pl.DeviceIdType.MESH,
        )

    def either(condition, act):
        pl.when(condition)(functools.partial(act, True))
        pl.when(jnp.logical_not(condition))(functools.partial(act, False))

    lane_x = lax.broadcasted_iota(jnp.int32, (cells_y, cells_x, mixed.shape[-1]), 1)

    for step in range(STEPS):
        source = adj_ref if step == 0 else mid
        target = mid if step < STEPS - 1 else out_ref

        if step == 0:
            loads[1].wait()
            loads[-1].wait()
        for s in range(species):
            base = s * slots
            if step == 0:
                loads[2 + s].wait()
            values = source[pl.ds(base, slots)].reshape(slots * cells_y * cells_x, -1)
            high = values.astype(jnp.bfloat16)
            low = (values - high.astype(jnp.float32)).astype(jnp.bfloat16)
            inverse = inverse_ref[s]
            inverse_high = inverse.astype(jnp.bfloat16)
            inverse_low = (inverse - inverse_high.astype(jnp.float32)).astype(jnp.bfloat16)
            both = jnp.concatenate([inverse_high, inverse_low], axis=1)
            product = jnp.dot(
                jnp.concatenate([high, low], axis=1),
                jnp.concatenate([both, both], axis=0),
                preferred_element_type=jnp.float32,
            )
            levels = inverse.shape[-1]
            product = product[:, :levels] + product[:, levels:]
            mixed[pl.ds(base, slots)] = product.reshape(slots, cells_y * cells_x, levels)
            for k in range(slots):
                for side in range(4):
                    strip = strips[side]
                    flux = courant_ref[side // 2, k, strip, :] * mixed[base + k, strip, :]
                    outgoing(step, side)[base + k] = flux

        for side in range(4):

            @pl.when(seam[side])
            def _(side=side):
                strip, face = strips[side], seam_faces[side]
                factor = courant_ref[side // 2, face, strip, :]
                for s in range(species):
                    outgoing(step, side)[s] = factor * mixed[s * slots + face, strip, :]

        @pl.when(at_north)
        def _():
            factor = courant_ref[1, face_y, last_row, :]
            for s in range(species):
                to_turn_n[step][s] = factor * mixed[s * slots + face_y, last_row, :]

        @pl.when(at_east)
        def _():
            for j in range(ratio):
                strip = pl.ds(j * cells_x * cells_x + cells_x - 1, cells_x, stride=cells_x)
                factor = courant_ref[0, face_z, strip, :]
                for s in range(species):
                    to_turn_e[step][j][s] = factor * mixed[s * slots + face_z, strip, :]

        if step == 0:
            peers = 4 + sum(c.astype(jnp.int32) for c in [north_remote, *east_remote])
            pl.semaphore_wait(barrier, peers)

        for j in range(ratio):

            @pl.when(north_remote & (turn_part == j))
            def _(j=j):
                north_copy(step, j).start()

            @pl.when(east_remote[j])
            def _(j=j):
                east_copy(step, j).start()

        for side in range(4):
            either(seam[side], lambda short, side=side: halo_copy(step, side, short).start())

        @pl.when(corner)
        def _():
            from_turn_e[step][ratio - 1][...] = to_turn_n[step][...]
            from_turn_n[step][...] = to_turn_e[step][ratio - 1][...]

        for s in range(species):
            for k in range(slots):
                here = mixed[s * slots + k].reshape(cells_y, cells_x, -1)
                along_x = 0.5 * courant_ref[0, k].reshape(here.shape) * here
                along_y = 0.5 * courant_ref[1, k].reshape(here.shape) * here
                ahead = jnp.where(
                    lane_x == cells_x - 1, 0.0, pltpu.roll(along_x, cells_x - 1, 1)
                )
                behind = jnp.where(lane_x == 0, 0.0, pltpu.roll(along_x, 1, 1))
                nothing = jnp.zeros_like(along_y[:1])
                above = jnp.concatenate([along_y[1:], nothing], axis=0)
                below = jnp.concatenate([nothing, along_y[:-1]], axis=0)
                result = here + (ahead - behind) + (above - below)
                target[s * slots + k] = result.reshape(cells_y * cells_x, -1)

        for side in range(4):
            either(
                far_seam[side], lambda short, side=side: halo_copy(step, side, short).wait_recv()
            )

        @pl.when(at_east)
        def _():
            for j in range(ratio):
                if j < ratio - 1:
                    north_copy(step, j).wait_recv()
                else:

                    @pl.when(east_remote[j])
                    def _():
                        north_copy(step, ratio - 1).wait_recv()

        @pl.when(north_remote)
        def _():
            east_copy(step, 0).wait_recv()

        boundary = (first_col, last_col, first_row, last_row)
        sign = (-0.5, 0.5, -0.5, 0.5)
        filled = (face_y, face_x, face_z, face_x)
        for side in range(4):
            strip = boundary[side]

            @pl.when(jnp.logical_not(far_seam[side]))
            def _(side=side, strip=strip):
                for s in range(species):
                    for k in range(slots):
                        index = s * slots + k
                        ghost = incoming(step, side)[index]
                        target[index, strip, :] = target[index, strip, :] + sign[side] * ghost

            @pl.when(far_seam[side])
            def _(side=side, strip=strip):
                for s in range(species):
                    ghost = incoming(step, side)[s]
                    for k in range(slots):
                        index = s * slots + k
                        value = target[index, strip, :]
                        value = value + weight(filled[side], k, sign[side]) * ghost
                        if side == WEST:
                            turned = jnp.concatenate(
                                [from_turn_e[step][j][s] for j in range(ratio)], axis=0
                            )
                            value = value - weight(face_z, k, 0.5) * turned
                        if side == SOUTH:
                            value = value - weight(face_y, k, 0.5) * from_turn_n[step][s]
                        target[index, strip, :] = value

    for step in range(STEPS):
        for side in range(4):
            either(seam[side], lambda short, side=side: halo_copy(step, side, short).wait_send())

        for j in range(ratio):

            @pl.when(north_remote & (turn_part == j))
            def _(j=j):
                north_copy(step, j).wait_send()

            @pl.when(east_remote[j])
            def _(j=j):
                east_copy(step, j).wait_send()


def on_device(adjoint_in, courant, vertical_inverse, links):
    cols, rows = lax.axis_size("tx"), lax.axis_size("ty")
    species, slots, cells_y, cells_x, levels = adjoint_in.shape
    ratio = cells_y // cells_x
    planes, cells = species * slots, cells_y * cells_x

    def buffer(*shape):
        return pltpu.VMEM(shape + (levels,), jnp.float32)

    halo = [buffer(planes, cells_y)] * 2 + [buffer(planes, cells_x)] * 2
    turn = buffer(species, cells_x)
    result = pl.pallas_call(
        functools.partial(kernel, species, slots, cells_y, cells_x, cols, rows),
        out_shape=jax.ShapeDtypeStruct((planes, cells, levels), jnp.float32),
        in_specs=[pl.BlockSpec(memory_space=pltpu.HBM)] * 4,
        out_specs=pl.BlockSpec(memory_space=pltpu.VMEM),
        scratch_shapes=[
            buffer(planes, cells),
            buffer(2, slots, cells),
            buffer(species, levels),
            pltpu.SMEM(links.shape[::-1], jnp.int32),
            buffer(planes, cells),
            buffer(planes, cells),
            [halo] * STEPS,
            [halo] * STEPS,
            [turn] * STEPS,
            [[turn] * ratio] * STEPS,
            [[turn] * ratio] * STEPS,
            [turn] * STEPS,
            pltpu.SemaphoreType.DMA((STEPS, 4)),
            pltpu.SemaphoreType.DMA((STEPS, 4)),
            pltpu.SemaphoreType.DMA((STEPS, ratio + 1)),
            pltpu.SemaphoreType.DMA((STEPS, ratio + 1)),
            pltpu.SemaphoreType.DMA((species + 3,)),
        ],
        compiler_params=pltpu.CompilerParams(
            collective_id=0, has_side_effects=True, vmem_limit_bytes=56 * 1024 * 1024
        ),
    )(
        adjoint_in.reshape(planes, cells, levels),
        courant.reshape(2, slots, cells, levels),
        vertical_inverse,
        links.T,
    )
    return result.reshape(adjoint_in.shape)


def solution(mesh):
    placed = (P(None, None, "ty", "tx", None), P(None, None, "ty", "tx", None), P(), P())
    return jax.shard_map(
        on_device,
        mesh=mesh,
        in_specs=placed,
        out_specs=P(None, None, "ty", "tx", None),
        check_vma=False,
    )
```

```python
import functools

import jax
import jax.numpy as jnp
from jax import lax
from jax.experimental import pallas as pl
from jax.experimental.pallas import tpu as pltpu
from jax.sharding import PartitionSpec as P

STEPS = 2
EAST, WEST, NORTH, SOUTH = range(4)


def kernel(
    species, slots, cells_y, cells_x, cols, rows,
    adj_hbm, courant_hbm, inverse_hbm, links_hbm, out_ref,
    adj_ref, courant_ref, inverse_ref, links_ref,
    mid, mixed, sent, received, to_turn_n, to_turn_e, from_turn_e, from_turn_n,
    send_sems, recv_sems, turn_send, turn_recv, load_sems,
):
    ratio = cells_y // cells_x
    tile_count = cols * rows
    col = lax.axis_index("tx")
    row = lax.axis_index("ty")
    at_east, at_west = col == cols - 1, col == 0
    at_north, at_south = row == rows - 1, row == 0
    seam = (at_east, at_west, at_north, at_south)
    far_seam = (at_west, at_east, at_south, at_north)
    east, west = lax.rem(col + 1, cols), lax.rem(col + cols - 1, cols)
    north, south = lax.rem(row + 1, rows), lax.rem(row + rows - 1, rows)
    targets = ({"tx": east}, {"tx": west}, {"ty": north}, {"ty": south})
    turn_row = lax.div(col * cells_x, cells_y)
    turn_part = lax.rem(col, ratio)
    north_turns = {"tx": cols - 1, "ty": turn_row}
    north_remote = at_north & jnp.logical_not(at_east)
    east_turns = [{"tx": row * ratio + j, "ty": rows - 1} for j in range(ratio)]
    corner = at_east & at_north
    east_remote = [
        at_east & jnp.logical_not(at_north) if j == ratio - 1 else at_east for j in range(ratio)
    ]

    barrier = pltpu.get_barrier_semaphore()

    def greet(device):
        pl.semaphore_signal(
            barrier, inc=1, device_id=device, device_id_type=pl.DeviceIdType.MESH
        )

    for device in targets:
        greet(device)

    @pl.when(north_remote)
    def _():
        greet(north_turns)

    for j in range(ratio):

        @pl.when(east_remote[j])
        def _(j=j):
            greet(east_turns[j])

    loads = [
        pltpu.make_async_copy(links_hbm, links_ref, load_sems.at[0]),
        pltpu.make_async_copy(inverse_hbm, inverse_ref, load_sems.at[1]),
    ]
    for s in range(species):
        planes = pl.ds(s * slots, slots)
        loads.append(
            pltpu.make_async_copy(adj_hbm.at[planes], adj_ref.at[planes], load_sems.at[3 + s])
        )
    loads.append(pltpu.make_async_copy(courant_hbm, courant_ref, load_sems.at[2]))
    for load in loads:
        load.start()
    loads[0].wait()

    def read_link(index, tiles):
        turned = links_ref[3, index] == 2
        return (
            jnp.where(turned, links_ref[0, index], tiles[0]),
            jnp.where(turned, links_ref[1, index], tiles[1]),
        )

    zero = jnp.int32(0)
    tile_y, tile_z = lax.fori_loop(0, links_ref.shape[1], read_link, (zero, zero))
    face_y, face_z = lax.div(tile_y, tile_count), lax.div(tile_z, tile_count)
    face_x = jnp.clip(slots - face_y - face_z, 0, slots - 1)
    face_y = jnp.clip(face_y, 0, slots - 1)
    face_z = jnp.clip(face_z, 0, slots - 1)

    def weight(face, slot, value):
        return jnp.where(face == slot, jnp.float32(value), jnp.float32(0.0))

    first_col = pl.ds(0, cells_y, stride=cells_x)
    last_col = pl.ds(cells_x - 1, cells_y, stride=cells_x)
    first_row = pl.ds(0, cells_x)
    last_row = pl.ds((cells_y - 1) * cells_x, cells_x)
    strips = (last_col, first_col, last_row, first_row)
    seam_faces = (face_x, face_y, face_x, face_z)

    def outgoing(step, side):
        return sent[step][side]

    def incoming(step, side):
        return received[step][side]

    def halo_copy(step, side, short):
        source, target = outgoing(step, side), incoming(step, side)
        if short:
            source, target = source.at[pl.ds(0, species)], target.at[pl.ds(0, species)]
        return pltpu.make_async_remote_copy(
            src_ref=source,
            dst_ref=target,
            send_sem=send_sems.at[step, side],
            recv_sem=recv_sems.at[step, side],
            device_id=targets[side],
            device_id_type=pl.DeviceIdType.MESH,
        )

    def north_copy(step, part):
        return pltpu.make_async_remote_copy(
            src_ref=to_turn_n[step],
            dst_ref=from_turn_e[step][part],
            send_sem=turn_send.at[step, ratio],
            recv_sem=turn_recv.at[step, part],
            device_id=north_turns,
            device_id_type=pl.DeviceIdType.MESH,
        )

    def east_copy(step, part):
        return pltpu.make_async_remote_copy(
            src_ref=to_turn_e[step][part],
            dst_ref=from_turn_n[step],
            send_sem=turn_send.at[step, part],
            recv_sem=turn_recv.at[step, ratio],
            device_id=east_turns[part],
            device_id_type=pl.DeviceIdType.MESH,
        )

    def either(condition, act):
        pl.when(condition)(functools.partial(act, True))
        pl.when(jnp.logical_not(condition))(functools.partial(act, False))

    lane_x = lax.broadcasted_iota(jnp.int32, (cells_y, cells_x, mixed.shape[-1]), 1)

    for step in range(STEPS):
        source = adj_ref if step == 0 else mid
        target = mid if step < STEPS - 1 else out_ref

        if step == 0:
            loads[1].wait()
            loads[-1].wait()
        for s in range(species):
            base = s * slots
            if step == 0:
                loads[2 + s].wait()
            values = source[pl.ds(base, slots)].reshape(slots * cells_y * cells_x, -1)
            high = values.astype(jnp.bfloat16)
            low = (values - high.astype(jnp.float32)).astype(jnp.bfloat16)
            inverse = inverse_ref[s]
            inverse_high = inverse.astype(jnp.bfloat16)
            inverse_low = (inverse - inverse_high.astype(jnp.float32)).astype(jnp.bfloat16)
            both = jnp.concatenate([inverse_high, inverse_low], axis=1)
            product = jnp.dot(
                jnp.concatenate([high, low], axis=1),
                jnp.concatenate([both, both], axis=0),
                preferred_element_type=jnp.float32,
            )
            levels = inverse.shape[-1]
            product = product[:, :levels] + product[:, levels:]
            mixed[pl.ds(base, slots)] = product.reshape(slots, cells_y * cells_x, levels)
            for k in range(slots):
                for side in range(4):
                    strip = strips[side]
                    flux = courant_ref[side // 2, k, strip, :] * mixed[base + k, strip, :]
                    outgoing(step, side)[base + k] = flux

        for side in range(4):

            @pl.when(seam[side])
            def _(side=side):
                strip, face = strips[side], seam_faces[side]
                factor = courant_ref[side // 2, face, strip, :]
                for s in range(species):
                    outgoing(step, side)[s] = factor * mixed[s * slots + face, strip, :]

        @pl.when(at_north)
        def _():
            factor = courant_ref[1, face_y, last_row, :]
            for s in range(species):
                to_turn_n[step][s] = factor * mixed[s * slots + face_y, last_row, :]

        @pl.when(at_east)
        def _():
            for j in range(ratio):
                strip = pl.ds(j * cells_x * cells_x + cells_x - 1, cells_x, stride=cells_x)
                factor = courant_ref[0, face_z, strip, :]
                for s in range(species):
                    to_turn_e[step][j][s] = factor * mixed[s * slots + face_z, strip, :]

        if step == 0:
            peers = 4 + sum(c.astype(jnp.int32) for c in [north_remote, *east_remote])
            pl.semaphore_wait(barrier, peers)

        for j in range(ratio):

            @pl.when(north_remote & (turn_part == j))
            def _(j=j):
                north_copy(step, j).start()

            @pl.when(east_remote[j])
            def _(j=j):
                east_copy(step, j).start()

        for side in range(4):
            either(seam[side], lambda short, side=side: halo_copy(step, side, short).start())

        @pl.when(corner)
        def _():
            from_turn_e[step][ratio - 1][...] = to_turn_n[step][...]
            from_turn_n[step][...] = to_turn_e[step][ratio - 1][...]

        for s in range(species):
            for k in range(slots):
                here = mixed[s * slots + k].reshape(cells_y, cells_x, -1)
                along_x = 0.5 * courant_ref[0, k].reshape(here.shape) * here
                along_y = 0.5 * courant_ref[1, k].reshape(here.shape) * here
                ahead = jnp.where(
                    lane_x == cells_x - 1, 0.0, pltpu.roll(along_x, cells_x - 1, 1)
                )
                behind = jnp.where(lane_x == 0, 0.0, pltpu.roll(along_x, 1, 1))
                nothing = jnp.zeros_like(along_y[:1])
                above = jnp.concatenate([along_y[1:], nothing], axis=0)
                below = jnp.concatenate([nothing, along_y[:-1]], axis=0)
                result = here + (ahead - behind) + (above - below)
                target[s * slots + k] = result.reshape(cells_y * cells_x, -1)

        for side in range(4):
            either(
                far_seam[side], lambda short, side=side: halo_copy(step, side, short).wait_recv()
            )

        @pl.when(at_east)
        def _():
            for j in range(ratio):
                if j < ratio - 1:
                    north_copy(step, j).wait_recv()
                else:

                    @pl.when(east_remote[j])
                    def _():
                        north_copy(step, ratio - 1).wait_recv()

        @pl.when(north_remote)
        def _():
            east_copy(step, 0).wait_recv()

        boundary = (first_col, last_col, first_row, last_row)
        sign = (-0.5, 0.5, -0.5, 0.5)
        filled = (face_y, face_x, face_z, face_x)
        for side in range(4):
            strip = boundary[side]

            @pl.when(jnp.logical_not(far_seam[side]))
            def _(side=side, strip=strip):
                for s in range(species):
                    for k in range(slots):
                        index = s * slots + k
                        ghost = incoming(step, side)[index]
                        target[index, strip, :] = target[index, strip, :] + sign[side] * ghost

            @pl.when(far_seam[side])
            def _(side=side, strip=strip):
                for s in range(species):
                    ghost = incoming(step, side)[s]
                    for k in range(slots):
                        index = s * slots + k
                        value = target[index, strip, :]
                        value = value + weight(filled[side], k, sign[side]) * ghost
                        if side == WEST:
                            turned = jnp.concatenate(
                                [from_turn_e[step][j][s] for j in range(ratio)], axis=0
                            )
                            value = value - weight(face_z, k, 0.5) * turned
                        if side == SOUTH:
                            value = value - weight(face_y, k, 0.5) * from_turn_n[step][s]
                        target[index, strip, :] = value

    for step in range(STEPS):
        for side in range(4):
            either(seam[side], lambda short, side=side: halo_copy(step, side, short).wait_send())

        for j in range(ratio):

            @pl.when(north_remote & (turn_part == j))
            def _(j=j):
                north_copy(step, j).wait_send()

            @pl.when(east_remote[j])
            def _(j=j):
                east_copy(step, j).wait_send()


def on_device(adjoint_in, courant, vertical_inverse, links):
    cols, rows = lax.axis_size("tx"), lax.axis_size("ty")
    species, slots, cells_y, cells_x, levels = adjoint_in.shape
    ratio = cells_y // cells_x
    planes, cells = species * slots, cells_y * cells_x

    def buffer(*shape):
        return pltpu.VMEM(shape + (levels,), jnp.float32)

    halo = [buffer(planes, cells_y)] * 2 + [buffer(planes, cells_x)] * 2
    turn = buffer(species, cells_x)
    result = pl.pallas_call(
        functools.partial(kernel, species, slots, cells_y, cells_x, cols, rows),
        out_shape=buffer(planes, cells),
        in_specs=[pl.BlockSpec(memory_space=pltpu.HBM)] * 4,
        out_specs=pl.BlockSpec(memory_space=pltpu.VMEM),
        scratch_shapes=[
            buffer(planes, cells),
            buffer(2, slots, cells),
            buffer(species, levels),
            pltpu.SMEM(links.shape[::-1], jnp.int32),
            buffer(planes, cells),
            buffer(planes, cells),
            [halo] * STEPS,
            [halo] * STEPS,
            [turn] * STEPS,
            [[turn] * ratio] * STEPS,
            [[turn] * ratio] * STEPS,
            [turn] * STEPS,
            pltpu.SemaphoreType.DMA((STEPS, 4)),
            pltpu.SemaphoreType.DMA((STEPS, 4)),
            pltpu.SemaphoreType.DMA((STEPS, ratio + 1)),
            pltpu.SemaphoreType.DMA((STEPS, ratio + 1)),
            pltpu.SemaphoreType.DMA((species + 3,)),
        ],
        compiler_params=pltpu.CompilerParams(
            collective_id=0, has_side_effects=True, vmem_limit_bytes=54600 * 1024
        ),
    )(
        adjoint_in.reshape(planes, cells, levels),
        courant.reshape(2, slots, cells, levels),
        vertical_inverse,
        links.T,
    )
    return result.reshape(adjoint_in.shape)


def solution(mesh):
    placed = (P(None, None, "ty", "tx", None), P(None, None, "ty", "tx", None), P(), P())
    return jax.shard_map(
        on_device,
        mesh=mesh,
        in_specs=placed,
        out_specs=P(None, None, "ty", "tx", None),
        check_vma=False,
    )
```

```python
import functools

import jax
import jax.numpy as jnp
from jax import lax
from jax.experimental import pallas as pl
from jax.experimental.pallas import tpu as pltpu
from jax.sharding import PartitionSpec as P

STEPS = 2
EAST, WEST, NORTH, SOUTH = range(4)


def kernel(
    species, slots, cells_y, cells_x, cols, rows,
    adj_hbm, courant_hbm, inverse_hbm, links_hbm, out_ref,
    adj_ref, courant_ref, inverse_ref, links_ref,
    edges, mixed, sent, received, to_turn_n, to_turn_e, from_turn_e, from_turn_n,
    send_sems, recv_sems, turn_send, turn_recv, load_sems,
):
    ratio = cells_y // cells_x
    tile_count = cols * rows
    col = lax.axis_index("tx")
    row = lax.axis_index("ty")
    at_east, at_west = col == cols - 1, col == 0
    at_north, at_south = row == rows - 1, row == 0
    seam = (at_east, at_west, at_north, at_south)
    far_seam = (at_west, at_east, at_south, at_north)
    east, west = lax.rem(col + 1, cols), lax.rem(col + cols - 1, cols)
    north, south = lax.rem(row + 1, rows), lax.rem(row + rows - 1, rows)
    targets = ({"tx": east}, {"tx": west}, {"ty": north}, {"ty": south})
    turn_row = lax.div(col * cells_x, cells_y)
    turn_part = lax.rem(col, ratio)
    north_turns = {"tx": cols - 1, "ty": turn_row}
    north_remote = at_north & jnp.logical_not(at_east)
    east_turns = [{"tx": row * ratio + j, "ty": rows - 1} for j in range(ratio)]
    corner = at_east & at_north
    east_remote = [
        at_east & jnp.logical_not(at_north) if j == ratio - 1 else at_east for j in range(ratio)
    ]

    barrier = pltpu.get_barrier_semaphore()

    def greet(device):
        pl.semaphore_signal(
            barrier, inc=1, device_id=device, device_id_type=pl.DeviceIdType.MESH
        )

    for device in targets:
        greet(device)

    @pl.when(north_remote)
    def _():
        greet(north_turns)

    for j in range(ratio):

        @pl.when(east_remote[j])
        def _(j=j):
            greet(east_turns[j])

    loads = [
        pltpu.make_async_copy(links_hbm, links_ref, load_sems.at[0]),
        pltpu.make_async_copy(inverse_hbm, inverse_ref, load_sems.at[1]),
    ]
    for s in range(species):
        planes = pl.ds(s * slots, slots)
        loads.append(
            pltpu.make_async_copy(adj_hbm.at[planes], adj_ref.at[planes], load_sems.at[3 + s])
        )
    courant_load = pltpu.make_async_copy(courant_hbm, courant_ref, load_sems.at[2])
    for load in [*loads[:3], courant_load, *loads[3:]]:
        load.start()
    loads[0].wait()

    def read_link(index, tiles):
        turned = links_ref[3, index] == 2
        return (
            jnp.where(turned, links_ref[0, index], tiles[0]),
            jnp.where(turned, links_ref[1, index], tiles[1]),
        )

    zero = jnp.int32(0)
    tile_y, tile_z = lax.fori_loop(0, links_ref.shape[1], read_link, (zero, zero))
    face_y, face_z = lax.div(tile_y, tile_count), lax.div(tile_z, tile_count)
    face_x = jnp.clip(slots - face_y - face_z, 0, slots - 1)
    face_y = jnp.clip(face_y, 0, slots - 1)
    face_z = jnp.clip(face_z, 0, slots - 1)

    def weight(face, slot, value):
        return jnp.where(face == slot, jnp.float32(value), jnp.float32(0.0))

    first_col = pl.ds(0, cells_y, stride=cells_x)
    last_col = pl.ds(cells_x - 1, cells_y, stride=cells_x)
    first_row = pl.ds(0, cells_x)
    last_row = pl.ds((cells_y - 1) * cells_x, cells_x)
    strips = (last_col, first_col, last_row, first_row)
    seam_faces = (face_x, face_y, face_x, face_z)

    def outgoing(step, side):
        return sent[step][side]

    def incoming(step, side):
        return received[step][side]

    def halo_copy(step, side, short):
        source, target = outgoing(step, side), incoming(step, side)
        if short:
            source, target = source.at[pl.ds(0, species)], target.at[pl.ds(0, species)]
        return pltpu.make_async_remote_copy(
            src_ref=source,
            dst_ref=target,
            send_sem=send_sems.at[step, side],
            recv_sem=recv_sems.at[step, side],
            device_id=targets[side],
            device_id_type=pl.DeviceIdType.MESH,
        )

    def north_copy(step, part):
        return pltpu.make_async_remote_copy(
            src_ref=to_turn_n[step],
            dst_ref=from_turn_e[step][part],
            send_sem=turn_send.at[step, ratio],
            recv_sem=turn_recv.at[step, part],
            device_id=north_turns,
            device_id_type=pl.DeviceIdType.MESH,
        )

    def east_copy(step, part):
        return pltpu.make_async_remote_copy(
            src_ref=to_turn_e[step][part],
            dst_ref=from_turn_n[step],
            send_sem=turn_send.at[step, part],
            recv_sem=turn_recv.at[step, ratio],
            device_id=east_turns[part],
            device_id_type=pl.DeviceIdType.MESH,
        )

    def either(condition, act):
        pl.when(condition)(functools.partial(act, True))
        pl.when(jnp.logical_not(condition))(functools.partial(act, False))

    lane_x = lax.broadcasted_iota(jnp.int32, (cells_y, cells_x, mixed.shape[-1]), 1)

    cells, levels = cells_y * cells_x, mixed.shape[-1]
    boundary = (first_col, last_col, first_row, last_row)
    lengths = (cells_y, cells_y, cells_x, cells_x)
    starts = [slots * sum(lengths[:side]) for side in range(4)]

    def apply(s, values):
        high = values.astype(jnp.bfloat16)
        low = (values - high.astype(jnp.float32)).astype(jnp.bfloat16)
        inverse = inverse_ref[s]
        inverse_high = inverse.astype(jnp.bfloat16)
        inverse_low = (inverse - inverse_high.astype(jnp.float32)).astype(jnp.bfloat16)
        both = jnp.concatenate([inverse_high, inverse_low], axis=1)
        product = jnp.dot(
            jnp.concatenate([high, low], axis=1),
            jnp.concatenate([both, both], axis=0),
            preferred_element_type=jnp.float32,
        )
        return product[:, :levels] + product[:, levels:]

    for step in range(STEPS):
        last = step == STEPS - 1

        if step == 0:
            loads[1].wait()
            courant_load.wait()
        for s in range(species):
            base = s * slots
            if step == 0:
                loads[2 + s].wait()
            if step == 0:
                values = adj_ref[pl.ds(base, slots)].reshape(slots * cells, levels)
                mixed[pl.ds(base, slots)] = apply(s, values).reshape(slots, cells, levels)
            else:
                change = apply(s, edges[s])
                for side in range(4):
                    for k in range(slots):
                        place = starts[side] + k * lengths[side]
                        part = change[place : place + lengths[side]]
                        strip = boundary[side]
                        mixed[base + k, strip, :] = mixed[base + k, strip, :] + part
            for k in range(slots):
                for side in range(4):
                    strip = strips[side]
                    flux = courant_ref[side // 2, k, strip, :] * mixed[base + k, strip, :]
                    outgoing(step, side)[base + k] = flux

        for side in range(4):

            @pl.when(seam[side])
            def _(side=side):
                strip, face = strips[side], seam_faces[side]
                factor = courant_ref[side // 2, face, strip, :]
                for s in range(species):
                    outgoing(step, side)[s] = factor * mixed[s * slots + face, strip, :]

        @pl.when(at_north)
        def _():
            factor = courant_ref[1, face_y, last_row, :]
            for s in range(species):
                to_turn_n[step][s] = factor * mixed[s * slots + face_y, last_row, :]

        @pl.when(at_east)
        def _():
            for j in range(ratio):
                strip = pl.ds(j * cells_x * cells_x + cells_x - 1, cells_x, stride=cells_x)
                factor = courant_ref[0, face_z, strip, :]
                for s in range(species):
                    to_turn_e[step][j][s] = factor * mixed[s * slots + face_z, strip, :]

        if step == 0:
            peers = 4 + sum(c.astype(jnp.int32) for c in [north_remote, *east_remote])
            pl.semaphore_wait(barrier, peers)

        for j in range(ratio):

            @pl.when(north_remote & (turn_part == j))
            def _(j=j):
                north_copy(step, j).start()

            @pl.when(east_remote[j])
            def _(j=j):
                east_copy(step, j).start()

        for side in range(4):
            either(seam[side], lambda short, side=side: halo_copy(step, side, short).start())

        @pl.when(corner)
        def _():
            from_turn_e[step][ratio - 1][...] = to_turn_n[step][...]
            from_turn_n[step][...] = to_turn_e[step][ratio - 1][...]

        for s in range(species):
            results = []
            for k in range(slots):
                here = mixed[s * slots + k].reshape(cells_y, cells_x, -1)
                along_x = 0.5 * courant_ref[0, k].reshape(here.shape) * here
                along_y = 0.5 * courant_ref[1, k].reshape(here.shape) * here
                ahead = jnp.where(
                    lane_x == cells_x - 1, 0.0, pltpu.roll(along_x, cells_x - 1, 1)
                )
                behind = jnp.where(lane_x == 0, 0.0, pltpu.roll(along_x, 1, 1))
                nothing = jnp.zeros_like(along_y[:1])
                above = jnp.concatenate([along_y[1:], nothing], axis=0)
                below = jnp.concatenate([nothing, along_y[:-1]], axis=0)
                result = here + (ahead - behind) + (above - below)
                results.append(result.reshape(cells, levels))
                if last:
                    out_ref[s * slots + k] = results[-1]
            if not last:
                product = apply(s, jnp.concatenate(results, axis=0))
                mixed[pl.ds(s * slots, slots)] = product.reshape(slots, cells, levels)

        for side in range(4):
            either(
                far_seam[side], lambda short, side=side: halo_copy(step, side, short).wait_recv()
            )

        @pl.when(at_east)
        def _():
            for j in range(ratio):
                if j < ratio - 1:
                    north_copy(step, j).wait_recv()
                else:

                    @pl.when(east_remote[j])
                    def _():
                        north_copy(step, ratio - 1).wait_recv()

        @pl.when(north_remote)
        def _():
            east_copy(step, 0).wait_recv()

        sign = (-0.5, 0.5, -0.5, 0.5)
        def add(s, k, side, value):
            if last:
                index, strip = s * slots + k, boundary[side]
                out_ref[index, strip, :] = out_ref[index, strip, :] + value
            else:
                place = pl.ds(starts[side] + k * lengths[side], lengths[side])
                edges[s, place, :] = value

        filled = (face_y, face_x, face_z, face_x)
        for side in range(4):
            @pl.when(jnp.logical_not(far_seam[side]))
            def _(side=side):
                for s in range(species):
                    for k in range(slots):
                        index = s * slots + k
                        add(s, k, side, sign[side] * incoming(step, side)[index])

            @pl.when(far_seam[side])
            def _(side=side):
                for s in range(species):
                    ghost = incoming(step, side)[s]
                    for k in range(slots):
                        value = weight(filled[side], k, sign[side]) * ghost
                        if side == WEST:
                            turned = jnp.concatenate(
                                [from_turn_e[step][j][s] for j in range(ratio)], axis=0
                            )
                            value = value - weight(face_z, k, 0.5) * turned
                        if side == SOUTH:
                            value = value - weight(face_y, k, 0.5) * from_turn_n[step][s]
                        add(s, k, side, value)

    for step in range(STEPS):
        for side in range(4):
            either(seam[side], lambda short, side=side: halo_copy(step, side, short).wait_send())

        for j in range(ratio):

            @pl.when(north_remote & (turn_part == j))
            def _(j=j):
                north_copy(step, j).wait_send()

            @pl.when(east_remote[j])
            def _(j=j):
                east_copy(step, j).wait_send()


def on_device(adjoint_in, courant, vertical_inverse, links):
    cols, rows = lax.axis_size("tx"), lax.axis_size("ty")
    species, slots, cells_y, cells_x, levels = adjoint_in.shape
    ratio = cells_y // cells_x
    planes, cells = species * slots, cells_y * cells_x

    def buffer(*shape):
        return pltpu.VMEM(shape + (levels,), jnp.float32)

    halo = [buffer(planes, cells_y)] * 2 + [buffer(planes, cells_x)] * 2
    turn = buffer(species, cells_x)
    result = pl.pallas_call(
        functools.partial(kernel, species, slots, cells_y, cells_x, cols, rows),
        out_shape=buffer(planes, cells),
        in_specs=[pl.BlockSpec(memory_space=pltpu.HBM)] * 4,
        out_specs=pl.BlockSpec(memory_space=pltpu.VMEM),
        scratch_shapes=[
            buffer(planes, cells),
            buffer(2, slots, cells),
            buffer(species, levels),
            pltpu.SMEM(links.shape[::-1], jnp.int32),
            buffer(species, slots * 2 * (cells_y + cells_x)),
            buffer(planes, cells),
            [halo] * STEPS,
            [halo] * STEPS,
            [turn] * STEPS,
            [[turn] * ratio] * STEPS,
            [[turn] * ratio] * STEPS,
            [turn] * STEPS,
            pltpu.SemaphoreType.DMA((STEPS, 4)),
            pltpu.SemaphoreType.DMA((STEPS, 4)),
            pltpu.SemaphoreType.DMA((STEPS, ratio + 1)),
            pltpu.SemaphoreType.DMA((STEPS, ratio + 1)),
            pltpu.SemaphoreType.DMA((species + 3,)),
        ],
        compiler_params=pltpu.CompilerParams(
            collective_id=0, has_side_effects=True, vmem_limit_bytes=54600 * 1024
        ),
    )(
        adjoint_in.reshape(planes, cells, levels),
        courant.reshape(2, slots, cells, levels),
        vertical_inverse,
        links.T,
    )
    return result.reshape(adjoint_in.shape)


def solution(mesh):
    placed = (P(None, None, "ty", "tx", None), P(None, None, "ty", "tx", None), P(), P())
    return jax.shard_map(
        on_device,
        mesh=mesh,
        in_specs=placed,
        out_specs=P(None, None, "ty", "tx", None),
        check_vma=False,
    )
```

```python
import functools

import jax
import jax.numpy as jnp
from jax import lax
from jax.experimental import pallas as pl
from jax.experimental.pallas import tpu as pltpu
from jax.sharding import PartitionSpec as P

STEPS = 2
EAST, WEST, NORTH, SOUTH = range(4)


def kernel(
    species, slots, cells_y, cells_x, cols, rows,
    adj_hbm, courant_hbm, inverse_hbm, links_hbm, out_ref,
    adj_ref, courant_ref, inverse_ref, links_ref,
    edges, mixed, sent, received, to_turn_n, to_turn_e, from_turn_e, from_turn_n,
    send_sems, recv_sems, turn_send, turn_recv, load_sems,
):
    ratio = cells_y // cells_x
    tile_count = cols * rows
    col = lax.axis_index("tx")
    row = lax.axis_index("ty")
    at_east, at_west = col == cols - 1, col == 0
    at_north, at_south = row == rows - 1, row == 0
    seam = (at_east, at_west, at_north, at_south)
    far_seam = (at_west, at_east, at_south, at_north)
    east, west = lax.rem(col + 1, cols), lax.rem(col + cols - 1, cols)
    north, south = lax.rem(row + 1, rows), lax.rem(row + rows - 1, rows)
    targets = ({"tx": east}, {"tx": west}, {"ty": north}, {"ty": south})
    turn_row = lax.div(col * cells_x, cells_y)
    turn_part = lax.rem(col, ratio)
    north_turns = {"tx": cols - 1, "ty": turn_row}
    north_remote = at_north & jnp.logical_not(at_east)
    east_turns = [{"tx": row * ratio + j, "ty": rows - 1} for j in range(ratio)]
    corner = at_east & at_north
    east_remote = [
        at_east & jnp.logical_not(at_north) if j == ratio - 1 else at_east for j in range(ratio)
    ]

    barrier = pltpu.get_barrier_semaphore()

    def greet(device):
        pl.semaphore_signal(
            barrier, inc=1, device_id=device, device_id_type=pl.DeviceIdType.MESH
        )

    for device in targets:
        greet(device)

    @pl.when(north_remote)
    def _():
        greet(north_turns)

    for j in range(ratio):

        @pl.when(east_remote[j])
        def _(j=j):
            greet(east_turns[j])

    loads = [
        pltpu.make_async_copy(links_hbm, links_ref, load_sems.at[0]),
        pltpu.make_async_copy(inverse_hbm.at[0], inverse_ref.at[0], load_sems.at[1]),
    ]
    for s in range(species):
        planes = pl.ds(s * slots, slots)
        loads.append(
            pltpu.make_async_copy(adj_hbm.at[planes], adj_ref.at[planes], load_sems.at[3 + s])
        )
    courant_load = pltpu.make_async_copy(courant_hbm, courant_ref, load_sems.at[2])
    inverse_loads = loads[1:2] + [
        pltpu.make_async_copy(inverse_hbm.at[s], inverse_ref.at[s], load_sems.at[2 + species + s])
        for s in range(1, species)
    ]
    for load in [*loads[:3], courant_load]:
        load.start()
    for s in range(1, species):
        inverse_loads[s].start()
        loads[2 + s].start()
    loads[0].wait()

    def read_link(index, tiles):
        turned = links_ref[3, index] == 2
        return (
            jnp.where(turned, links_ref[0, index], tiles[0]),
            jnp.where(turned, links_ref[1, index], tiles[1]),
        )

    zero = jnp.int32(0)
    tile_y, tile_z = lax.fori_loop(0, links_ref.shape[1], read_link, (zero, zero))
    face_y, face_z = lax.div(tile_y, tile_count), lax.div(tile_z, tile_count)
    face_x = jnp.clip(slots - face_y - face_z, 0, slots - 1)
    face_y = jnp.clip(face_y, 0, slots - 1)
    face_z = jnp.clip(face_z, 0, slots - 1)

    def weight(face, slot, value):
        return jnp.where(face == slot, jnp.float32(value), jnp.float32(0.0))

    first_col = pl.ds(0, cells_y, stride=cells_x)
    last_col = pl.ds(cells_x - 1, cells_y, stride=cells_x)
    first_row = pl.ds(0, cells_x)
    last_row = pl.ds((cells_y - 1) * cells_x, cells_x)
    strips = (last_col, first_col, last_row, first_row)
    seam_faces = (face_x, face_y, face_x, face_z)

    def outgoing(step, side):
        return sent[step][side]

    def incoming(step, side):
        return received[step][side]

    def halo_copy(step, side, short):
        source, target = outgoing(step, side), incoming(step, side)
        if short:
            source, target = source.at[pl.ds(0, species)], target.at[pl.ds(0, species)]
        return pltpu.make_async_remote_copy(
            src_ref=source,
            dst_ref=target,
            send_sem=send_sems.at[step, side],
            recv_sem=recv_sems.at[step, side],
            device_id=targets[side],
            device_id_type=pl.DeviceIdType.MESH,
        )

    def north_copy(step, part):
        return pltpu.make_async_remote_copy(
            src_ref=to_turn_n[step],
            dst_ref=from_turn_e[step][part],
            send_sem=turn_send.at[step, ratio],
            recv_sem=turn_recv.at[step, part],
            device_id=north_turns,
            device_id_type=pl.DeviceIdType.MESH,
        )

    def east_copy(step, part):
        return pltpu.make_async_remote_copy(
            src_ref=to_turn_e[step][part],
            dst_ref=from_turn_n[step],
            send_sem=turn_send.at[step, part],
            recv_sem=turn_recv.at[step, ratio],
            device_id=east_turns[part],
            device_id_type=pl.DeviceIdType.MESH,
        )

    def either(condition, act):
        pl.when(condition)(functools.partial(act, True))
        pl.when(jnp.logical_not(condition))(functools.partial(act, False))

    lane_x = lax.broadcasted_iota(jnp.int32, (cells_y, cells_x, mixed.shape[-1]), 1)

    cells, levels = cells_y * cells_x, mixed.shape[-1]
    boundary = (first_col, last_col, first_row, last_row)
    lengths = (cells_y, cells_y, cells_x, cells_x)
    starts = [slots * sum(lengths[:side]) for side in range(4)]

    def apply(s, values):
        high = values.astype(jnp.bfloat16)
        low = (values - high.astype(jnp.float32)).astype(jnp.bfloat16)
        inverse = inverse_ref[s]
        inverse_high = inverse.astype(jnp.bfloat16)
        inverse_low = (inverse - inverse_high.astype(jnp.float32)).astype(jnp.bfloat16)
        both = jnp.concatenate([inverse_high, inverse_low], axis=1)
        product = jnp.dot(
            jnp.concatenate([high, low], axis=1),
            jnp.concatenate([both, both], axis=0),
            preferred_element_type=jnp.float32,
        )
        return product[:, :levels] + product[:, levels:]

    for step in range(STEPS):
        last = step == STEPS - 1

        if step == 0:
            courant_load.wait()
        for s in range(species):
            base = s * slots
            if step == 0:
                inverse_loads[s].wait()
                loads[2 + s].wait()
            if step == 0:
                values = adj_ref[pl.ds(base, slots)].reshape(slots * cells, levels)
                mixed[pl.ds(base, slots)] = apply(s, values).reshape(slots, cells, levels)
            else:
                change = apply(s, edges[s])
                for side in range(4):
                    for k in range(slots):
                        place = starts[side] + k * lengths[side]
                        part = change[place : place + lengths[side]]
                        strip = boundary[side]
                        mixed[base + k, strip, :] = mixed[base + k, strip, :] + part
            for k in range(slots):
                for side in range(4):
                    strip = strips[side]
                    flux = courant_ref[side // 2, k, strip, :] * mixed[base + k, strip, :]
                    outgoing(step, side)[base + k] = flux

        for side in range(4):

            @pl.when(seam[side])
            def _(side=side):
                strip, face = strips[side], seam_faces[side]
                factor = courant_ref[side // 2, face, strip, :]
                for s in range(species):
                    outgoing(step, side)[s] = factor * mixed[s * slots + face, strip, :]

        @pl.when(at_north)
        def _():
            factor = courant_ref[1, face_y, last_row, :]
            for s in range(species):
                to_turn_n[step][s] = factor * mixed[s * slots + face_y, last_row, :]

        @pl.when(at_east)
        def _():
            for j in range(ratio):
                strip = pl.ds(j * cells_x * cells_x + cells_x - 1, cells_x, stride=cells_x)
                factor = courant_ref[0, face_z, strip, :]
                for s in range(species):
                    to_turn_e[step][j][s] = factor * mixed[s * slots + face_z, strip, :]

        if step == 0:
            peers = 4 + sum(c.astype(jnp.int32) for c in [north_remote, *east_remote])
            pl.semaphore_wait(barrier, peers)

        for j in range(ratio):

            @pl.when(north_remote & (turn_part == j))
            def _(j=j):
                north_copy(step, j).start()

            @pl.when(east_remote[j])
            def _(j=j):
                east_copy(step, j).start()

        for side in range(4):
            either(seam[side], lambda short, side=side: halo_copy(step, side, short).start())

        @pl.when(corner)
        def _():
            from_turn_e[step][ratio - 1][...] = to_turn_n[step][...]
            from_turn_n[step][...] = to_turn_e[step][ratio - 1][...]

        for s in range(species):
            results = []
            for k in range(slots):
                here = mixed[s * slots + k].reshape(cells_y, cells_x, -1)
                along_x = 0.5 * courant_ref[0, k].reshape(here.shape) * here
                along_y = 0.5 * courant_ref[1, k].reshape(here.shape) * here
                ahead = jnp.where(
                    lane_x == cells_x - 1, 0.0, pltpu.roll(along_x, cells_x - 1, 1)
                )
                behind = jnp.where(lane_x == 0, 0.0, pltpu.roll(along_x, 1, 1))
                nothing = jnp.zeros_like(along_y[:1])
                above = jnp.concatenate([along_y[1:], nothing], axis=0)
                below = jnp.concatenate([nothing, along_y[:-1]], axis=0)
                result = here + (ahead - behind) + (above - below)
                results.append(result.reshape(cells, levels))
                if last:
                    out_ref[s * slots + k] = results[-1]
            if not last:
                product = apply(s, jnp.concatenate(results, axis=0))
                mixed[pl.ds(s * slots, slots)] = product.reshape(slots, cells, levels)

        for side in range(4):
            either(
                far_seam[side], lambda short, side=side: halo_copy(step, side, short).wait_recv()
            )

        @pl.when(at_east)
        def _():
            for j in range(ratio):
                if j < ratio - 1:
                    north_copy(step, j).wait_recv()
                else:

                    @pl.when(east_remote[j])
                    def _():
                        north_copy(step, ratio - 1).wait_recv()

        @pl.when(north_remote)
        def _():
            east_copy(step, 0).wait_recv()

        sign = (-0.5, 0.5, -0.5, 0.5)
        def add(s, k, side, value):
            if last:
                index, strip = s * slots + k, boundary[side]
                out_ref[index, strip, :] = out_ref[index, strip, :] + value
            else:
                place = pl.ds(starts[side] + k * lengths[side], lengths[side])
                edges[s, place, :] = value

        filled = (face_y, face_x, face_z, face_x)
        for side in range(4):
            @pl.when(jnp.logical_not(far_seam[side]))
            def _(side=side):
                for s in range(species):
                    for k in range(slots):
                        index = s * slots + k
                        add(s, k, side, sign[side] * incoming(step, side)[index])

            @pl.when(far_seam[side])
            def _(side=side):
                for s in range(species):
                    ghost = incoming(step, side)[s]
                    for k in range(slots):
                        value = weight(filled[side], k, sign[side]) * ghost
                        if side == WEST:
                            turned = jnp.concatenate(
                                [from_turn_e[step][j][s] for j in range(ratio)], axis=0
                            )
                            value = value - weight(face_z, k, 0.5) * turned
                        if side == SOUTH:
                            value = value - weight(face_y, k, 0.5) * from_turn_n[step][s]
                        add(s, k, side, value)

    for step in range(STEPS):
        for side in range(4):
            either(seam[side], lambda short, side=side: halo_copy(step, side, short).wait_send())

        for j in range(ratio):

            @pl.when(north_remote & (turn_part == j))
            def _(j=j):
                north_copy(step, j).wait_send()

            @pl.when(east_remote[j])
            def _(j=j):
                east_copy(step, j).wait_send()


def on_device(adjoint_in, courant, vertical_inverse, links):
    cols, rows = lax.axis_size("tx"), lax.axis_size("ty")
    species, slots, cells_y, cells_x, levels = adjoint_in.shape
    ratio = cells_y // cells_x
    planes, cells = species * slots, cells_y * cells_x

    def buffer(*shape):
        return pltpu.VMEM(shape + (levels,), jnp.float32)

    halo = [buffer(planes, cells_y)] * 2 + [buffer(planes, cells_x)] * 2
    turn = buffer(species, cells_x)
    result = pl.pallas_call(
        functools.partial(kernel, species, slots, cells_y, cells_x, cols, rows),
        out_shape=buffer(planes, cells),
        in_specs=[pl.BlockSpec(memory_space=pltpu.HBM)] * 4,
        out_specs=pl.BlockSpec(memory_space=pltpu.VMEM),
        scratch_shapes=[
            buffer(planes, cells),
            buffer(2, slots, cells),
            buffer(species, levels),
            pltpu.SMEM(links.shape[::-1], jnp.int32),
            buffer(species, slots * 2 * (cells_y + cells_x)),
            buffer(planes, cells),
            [halo] * STEPS,
            [halo] * STEPS,
            [turn] * STEPS,
            [[turn] * ratio] * STEPS,
            [[turn] * ratio] * STEPS,
            [turn] * STEPS,
            pltpu.SemaphoreType.DMA((STEPS, 4)),
            pltpu.SemaphoreType.DMA((STEPS, 4)),
            pltpu.SemaphoreType.DMA((STEPS, ratio + 1)),
            pltpu.SemaphoreType.DMA((STEPS, ratio + 1)),
            pltpu.SemaphoreType.DMA((2 * species + 2,)),
        ],
        compiler_params=pltpu.CompilerParams(
            collective_id=0, has_side_effects=True, vmem_limit_bytes=54600 * 1024
        ),
    )(
        adjoint_in.reshape(planes, cells, levels),
        courant.reshape(2, slots, cells, levels),
        vertical_inverse,
        links.T,
    )
    return result.reshape(adjoint_in.shape)


def solution(mesh):
    placed = (P(None, None, "ty", "tx", None), P(None, None, "ty", "tx", None), P(), P())
    return jax.shard_map(
        on_device,
        mesh=mesh,
        in_specs=placed,
        out_specs=P(None, None, "ty", "tx", None),
        check_vma=False,
    )
```
